32 devices in a mesh: scene: 2 (over y), row: 4 (over z), col: 2 (over x), mode: 2 (over core).
Axes of the slice: x: 2, y: 2, z: 4, core: 2. Of those that a mesh axis runs over, the one named last changes fastest.
Arguments:
- object_field: float32 [4, 2048, 1024], P('scene', 'row', 'col'), parts along dimension 0, may hold values from -4 to 4
- probe_modes: float32 [16, 2, 256, 256], P(('scene', 'mode')), parts along dimension 0, may hold values from -1 to 1
- amplitudes: float32 [8, 2, 2, 256, 256], P(('scene', 'row'), 'col'), parts along dimension 0, may hold values from 0.2 to 2
- positions: int32 [8, 2, 2, 2], P(('scene', 'row'), 'col'), parts along dimension 0, may hold values from 0 to 512, as said below
- counts: int32 [8, 2], P(('scene', 'row'), 'col'), parts along dimension 0, may hold values from 1 to 2, as said below
Outputs:
- object_grad: float32 [4, 2048, 1024], P(('scene', 'mode'), 'row', 'col'), parts along dimension 0
- probe_grad: float32 [16, 2, 256, 256], P(('scene', 'mode')), parts along dimension 0
The draws below stay inside these ranges and needn't reach their ends.
There are 2 independent parts, one for each index of `scene`. The reference program is written for one: setup_inputs(seed, part) draws one part's arguments, and reference() takes and returns one part's arrays. A program takes and returns all parts, laid end to end along the dimension named above; each array names one. Nothing has to cross between parts.
Inputs may be any that keep to these rules, and one draw needn't show every extreme that they name: `positions`: row and column offset of a slot's 256 x 256 patch in its tile's frame widened by 128 cells on every side; slots at or beyond the tile's count are ignored. Slots 0 to counts - 1 of a tile are live.
All inputs are finite; a program needn't handle non-finite values.
Results may differ from the reference program's by a relative error of at most 0.0075.
Values sent between devices are 32-bit elements; how exact they have to be, the bound alone decides.
No kernel may reach another device: no remote copies, remote signals or barrier semaphores. Data moves between devices by JAX's collectives and lax.ppermute only.
A program may use at most 128 MiB of HBM per device.

```python
import math
import jax
import jax.numpy as jnp
from jax import lax

TILE = 512
MAXPOS = 2
PROBE = 256
MODES = 8
HALO = 128
GRID_R = 4
GRID_C = 2
NY = 2048
NX = 1024


def draw_positions(key, part):
    key = jax.random.fold_in(key, 11)
    offsets = jax.random.randint(key, (GRID_R, GRID_C, MAXPOS, 2), 0, TILE + 1, dtype=jnp.int32)
    pick_key = jax.random.fold_in(key, 5)
    row_key, col_key = jax.random.split(pick_key)
    chosen_row = jax.random.randint(row_key, (), 0, GRID_R, dtype=jnp.int32)
    chosen_col = jax.random.randint(col_key, (), 0, GRID_C, dtype=jnp.int32)
    corner_pair = jnp.array([0, TILE], dtype=jnp.int32)
    return offsets.at[chosen_row, chosen_col, 0].set(corner_pair)


def draw_counts(key, part):
    key = jax.random.fold_in(key, 23)
    first_key, second_key, row_key, col_key = jax.random.split(key, 4)
    first_draw = jax.random.randint(first_key, (GRID_R, GRID_C), 0, MAXPOS, dtype=jnp.int32)
    second_draw = jax.random.randint(second_key, (GRID_R, GRID_C), 0, MAXPOS, dtype=jnp.int32)
    tile_counts = jnp.minimum(first_draw, second_draw) + 1
    chosen_row = jax.random.randint(row_key, (), 0, GRID_R, dtype=jnp.int32)
    chosen_col = jax.random.randint(col_key, (), 0, GRID_C, dtype=jnp.int32)
    tile_counts = tile_counts.at[(chosen_row + 1) % GRID_R, chosen_col].set(1)
    return tile_counts.at[chosen_row, chosen_col].set(MAXPOS)


def steps_of(stream_key, shape, cuts, smallest, top_value):
    loudness, own = 1.0, jax.random.fold_in(stream_key, 6)
    for axis_at, blocks in cuts:
        draws = jnp.exp(jax.random.uniform(jax.random.fold_in(own, axis_at), (blocks,), jnp.float32, smallest / len(cuts), top_value / len(cuts)))
        loudness = loudness * jnp.repeat(draws, shape[axis_at] // blocks).reshape([-1 if axis == axis_at else 1 for axis in range(len(shape))])
    return loudness


def gaussian(key, extent, width, limit, pieces=(), kind=jnp.bfloat16):
    values = jax.random.normal(key, extent, jnp.float32) * width
    if len(pieces) > 0:
        values = steps_of(key, extent, pieces, -0.22, 0.18) * values
    return jnp.clip(values, min=-limit, max=limit).astype(kind)


def setup_inputs(seed: int = 0, part: int = 0) -> dict:
    seeds = jax.random.split(jax.random.key(seed), 6)
    own_keys = jax.random.split(jax.random.fold_in(seeds[5], part), 6)
    return {
        "object_field": gaussian(own_keys[0], (2, NY, NX), 1.0, 4.0, ((1, 4), (2, 2)), jnp.float32),
        "probe_modes": gaussian(own_keys[1], (MODES, 2, PROBE, PROBE), 0.18, 1.0, ((0, 2),), jnp.float32),
        "amplitudes": jnp.clip(0.2 + 1.8 * jax.random.uniform(own_keys[2], (GRID_R, GRID_C, MAXPOS, PROBE, PROBE), jnp.float32) ** steps_of(own_keys[2], (GRID_R, GRID_C, MAXPOS, PROBE, PROBE), ((0, 4), (1, 2)), -0.2, 0.2), 0.2, 2.0),
        "positions": draw_positions(jax.random.fold_in(jax.random.fold_in(seeds[5], part), 71), part),
        "counts": draw_counts(jax.random.fold_in(jax.random.fold_in(seeds[5], part), 71), part),
    }


damping = 0.1

def dft_tables(patch_size, direction):
    indices = jnp.arange(patch_size, dtype=jnp.int32)
    product = indices[:, None] * indices[None, :] % patch_size
    angles = 2.0 * math.pi / patch_size * product.astype(jnp.float32)
    norm_scale = 1.0 / math.sqrt(patch_size)
    real_part = (jnp.cos(angles) * norm_scale).astype(jnp.bfloat16)
    imag_part = (-direction * jnp.sin(angles) * norm_scale).astype(jnp.bfloat16)
    upper_rows = jnp.stack([real_part, -imag_part], axis=1)
    lower_rows = jnp.stack([imag_part, real_part], axis=1)
    left_table = jnp.stack([upper_rows, lower_rows], axis=0)
    right_table = jnp.transpose(left_table, (2, 3, 0, 1))
    return (left_table, right_table)

def transform(wave_field, left_table, right_table):
    halfway = jnp.einsum('dick,mckj->mdij', left_table.astype(jnp.float32), wave_field.astype(jnp.float32), precision=lax.Precision.HIGHEST).astype(jnp.bfloat16)
    return jnp.einsum('mcij,cjdl->mdil', halfway.astype(jnp.float32), right_table.astype(jnp.float32), precision=lax.Precision.HIGHEST)

def complex_product(left_term, right_term):
    left_real, left_imag = (left_term[..., 0, :, :], left_term[..., 1, :, :])
    right_real, right_imag = (right_term[..., 0, :, :], right_term[..., 1, :, :])
    return jnp.stack([left_real * right_real - left_imag * right_imag, left_real * right_imag + left_imag * right_real], axis=-3)

def conj_product(left_term, right_term):
    left_real, left_imag = (left_term[..., 0, :, :], left_term[..., 1, :, :])
    right_real, right_imag = (right_term[..., 0, :, :], right_term[..., 1, :, :])
    return jnp.stack([left_real * right_real + left_imag * right_imag, left_real * right_imag - left_imag * right_real], axis=-3)

def forward_pass(patches, probe_modes, left_table, right_table):
    exit_wave = complex_product(probe_modes[None], patches[:, None]).astype(jnp.bfloat16)
    shape_all = exit_wave.shape
    flattened = exit_wave.reshape((-1,) + shape_all[2:])
    return transform(flattened, left_table, right_table).reshape(shape_all)

def backward_pass(spectrum, weight, patches, probe_modes, left_table, right_table):
    back_hat = (weight[:, None, None] * spectrum).astype(jnp.bfloat16)
    shape_all = back_hat.shape
    flattened = back_hat.reshape((-1,) + shape_all[2:])
    back_wave = transform(flattened, left_table, right_table).reshape(shape_all)
    object_terms = lax.optimization_barrier(jnp.sum(conj_product(probe_modes[None], back_wave), axis=1))
    probe_term = lax.optimization_barrier(jnp.sum(conj_product(patches[:, None], back_wave), axis=0))
    return (object_terms, probe_term)

def reference(object_field, probe_modes, amplitudes, positions, counts):
    forward_left, forward_right = dft_tables(PROBE, 1.0)
    inverse_left, inverse_right = dft_tables(PROBE, -1.0)
    padded = jnp.pad(object_field, ((0, 0), (HALO, HALO), (HALO, HALO)))
    anchor = jnp.zeros((), jnp.int32)
    total_items = GRID_R * GRID_C * MAXPOS
    flat_index = jnp.arange(total_items, dtype=jnp.int32)
    slot_ids = flat_index % MAXPOS
    tile_ids = flat_index // MAXPOS
    row_ids = tile_ids // GRID_C
    col_ids = tile_ids % GRID_C

    def visit_slot(running, visit_items):
        gradient_grid, probe_total = running
        tile_row, tile_col, slot_index = visit_items
        offset = positions[tile_row, tile_col, slot_index]
        row_start = (tile_row * TILE + offset[0]).astype(jnp.int32)
        col_start = (tile_col * TILE + offset[1]).astype(jnp.int32)
        patches = lax.dynamic_slice(padded, (anchor, row_start, col_start), (2, PROBE, PROBE))[None]
        active = (slot_index < counts[tile_row, tile_col]).astype(jnp.float32)
        spectrum = forward_pass(patches, probe_modes, forward_left, forward_right)
        total_power = lax.optimization_barrier(jnp.sum(spectrum * spectrum, axis=(1, 2)))
        weight = active * (1.0 - amplitudes[tile_row, tile_col, slot_index][None] / jnp.sqrt(total_power + damping))
        object_terms, probe_term = backward_pass(spectrum, weight, patches, probe_modes, inverse_left, inverse_right)
        current = lax.dynamic_slice(gradient_grid, (anchor, row_start, col_start), (2, PROBE, PROBE))
        gradient_grid = lax.dynamic_update_slice(gradient_grid, current + object_terms[0], (anchor, row_start, col_start))
        return ((gradient_grid, probe_total + probe_term), None)
    start_state = (jnp.zeros(padded.shape, jnp.float32), jnp.zeros(probe_modes.shape, jnp.float32))
    (gradient_grid, probe_total), _ = lax.scan(visit_slot, start_state, (row_ids, col_ids, slot_ids))
    object_grad = gradient_grid[:, HALO:HALO + NY, HALO:HALO + NX]
    probe_grad = probe_total * (1.0 / math.sqrt(GRID_R * GRID_C))
    return (object_grad, probe_grad)
```

```python
import functools
import math

import jax
import jax.numpy as jnp
import numpy as np
from jax import lax
from jax.experimental import pallas as pl
from jax.experimental.pallas import tpu as pltpu
from jax.sharding import PartitionSpec as P

damping = 0.1
LANES = 128
SUBLANES = 8
VMEM_BYTES = 32 * 1024 * 1024

f32 = jnp.float32
bf16 = jnp.bfloat16


def dft_blocks(size):
    index = np.arange(size, dtype=np.int64)
    angles = 2.0 * np.pi / size * (index[:, None] * index[None, :] % size)
    real = (np.cos(angles) / np.sqrt(size)).astype(np.float32).astype(bf16)
    imag = (-np.sin(angles) / np.sqrt(size)).astype(np.float32).astype(bf16)
    left = np.block([[real, -imag], [imag, real]])
    return left, np.ascontiguousarray(left.T)


def params():
    return pltpu.CompilerParams(vmem_limit_bytes=VMEM_BYTES)


def whole(shape):
    return pl.BlockSpec(shape, lambda *_: (0,) * len(shape))


def window_of(offset):
    base_row = pl.multiple_of(offset[0] // SUBLANES * SUBLANES, SUBLANES)
    base_col = pl.multiple_of(offset[1] // LANES * LANES, LANES)
    return base_row, base_col, offset[0] - base_row, offset[1] - base_col


def cut_kernel(size, margin, tile, slots, info, own, up, down, left, right, ul, ur, dl, dr, out, frame):
    low, high = slice(0, margin), slice(margin + tile, 2 * margin + tile)
    mid = slice(margin, margin + tile)
    has_left = info[1].astype(f32)
    has_right = info[2].astype(f32)
    frame[low, mid] = up[...]
    frame[high, mid] = down[...]
    frame[mid, mid] = own[...]
    frame[mid, low] = left[...] * has_left
    frame[mid, high] = right[...] * has_right
    frame[low, low] = ul[...] * has_left
    frame[low, high] = ur[...] * has_right
    frame[high, low] = dl[...] * has_left
    frame[high, high] = dr[...] * has_right
    rows, cols = size + SUBLANES, size + LANES
    for slot in range(slots):
        base_row, base_col, row, col = window_of((info[3 + 2 * slot], info[4 + 2 * slot]))
        window = frame[pl.ds(base_row, rows), pl.ds(base_col, cols)]
        window = pltpu.roll(window, rows - row, 0)[:size]
        window = pltpu.roll(window, cols - col, 1)[:, :size]
        out[slot] = window


def cut_patches(info, field, strips, size, slots):
    tile = field.shape[-1]
    margin = size // 2
    span = tile + 2 * margin
    kernel = functools.partial(cut_kernel, size, margin, tile, slots)
    return pl.pallas_call(
        kernel,
        grid_spec=pltpu.PrefetchScalarGridSpec(
            num_scalar_prefetch=1,
            grid=(1,),
            in_specs=[pl.BlockSpec((None, tile, tile), lambda i, info: (info[0], 0, 0))]
            + [whole(s.shape) for s in strips],
            out_specs=whole((slots, size, size)),
            scratch_shapes=[pltpu.VMEM((span + SUBLANES, span + LANES), f32)],
        ),
        out_shape=jax.ShapeDtypeStruct((slots, size, size), f32),
        compiler_params=params(),
        name="cut",
    )(info, field, *strips)


def as_slot_rows(wave, size, slots):
    return jnp.concatenate(
        [
            jnp.concatenate(
                [wave[c * size : (c + 1) * size, s * size : (s + 1) * size] for c in range(2)], axis=1
            )
            for s in range(slots)
        ],
        axis=0,
    )


def forward_kernel(size, slots, info, probe, mine, other, left, right, spectrum, power):
    first = info[0] == 0
    pr, pi = probe[0], probe[1]
    real, imag = [], []
    for s in range(slots):
        a, b = mine[s], other[s]
        qr, qi = jnp.where(first, a, b), jnp.where(first, b, a)
        real.append((pr * qr - pi * qi).astype(bf16))
        imag.append((pr * qi + pi * qr).astype(bf16))
    wave = jnp.concatenate([jnp.concatenate(real, axis=1), jnp.concatenate(imag, axis=1)], axis=0)
    half = jnp.dot(left[...], wave, preferred_element_type=f32).astype(bf16)
    full = jnp.dot(as_slot_rows(half, size, slots), right[...], preferred_element_type=f32)

    @pl.when(pl.program_id(0) == 0)
    def _():
        power[...] = jnp.zeros_like(power)

    for s in range(slots):
        rows = full[s * size : (s + 1) * size]
        spectrum[s] = rows
        power[s] += rows[:, :size] * rows[:, :size] + rows[:, size:] * rows[:, size:]


def forward(info, probes, mine, other, left, right):
    modes, _, size, _ = probes.shape
    slots = mine.shape[0]
    return pl.pallas_call(
        functools.partial(forward_kernel, size, slots),
        grid_spec=pltpu.PrefetchScalarGridSpec(
            num_scalar_prefetch=1,
            grid=(modes,),
            in_specs=[
                pl.BlockSpec((None, 2, size, size), lambda m, info: (m, 0, 0, 0)),
                whole(mine.shape),
                whole(other.shape),
                whole(left.shape),
                whole(right.shape),
            ],
            out_specs=[
                pl.BlockSpec((None, slots, size, 2 * size), lambda m, info: (m, 0, 0, 0)),
                whole((slots, size, size)),
            ],
        ),
        out_shape=[
            jax.ShapeDtypeStruct((modes, slots, size, 2 * size), f32),
            jax.ShapeDtypeStruct((slots, size, size), f32),
        ],
        compiler_params=params(),
        name="forward",
    )(info, probes, mine, other, left, right)


def backward_kernel(
    size, slots, scale, info, probe, mine, other, amplitudes, power, power_other, spectrum, left, right,
    probe_keep, probe_send, object_keep, object_send, weight,
):
    step = pl.program_id(0)
    first = info[0] == 0
    low = info[1] == 0

    @pl.when(step == 0)
    def _():
        for s in range(slots):
            active = (s < info[2]).astype(f32)
            total = power[s] + power_other[s]
            weight[s] = active * (1.0 - amplitudes[s] / jnp.sqrt(total + damping))
        object_keep[...] = jnp.zeros_like(object_keep)
        object_send[...] = jnp.zeros_like(object_send)

    real, imag = [], []
    for s in range(slots):
        w = weight[s]
        real.append((w * spectrum[s, :, :size]).astype(bf16))
        imag.append((w * spectrum[s, :, size:]).astype(bf16))
    hat = jnp.concatenate([jnp.concatenate(real, axis=1), jnp.concatenate(imag, axis=1)], axis=0)
    half = jnp.dot(right[...], hat, preferred_element_type=f32).astype(bf16)
    back = jnp.dot(as_slot_rows(half, size, slots), left[...], preferred_element_type=f32)

    pr, pi = probe[0], probe[1]
    sum_real = jnp.zeros((size, size), f32)
    sum_imag = jnp.zeros((size, size), f32)
    for s in range(slots):
        br = back[s * size : (s + 1) * size, :size]
        bi = back[s * size : (s + 1) * size, size:]
        a, b = mine[s], other[s]
        qr, qi = jnp.where(first, a, b), jnp.where(first, b, a)
        sum_real += qr * br + qi * bi
        sum_imag += qr * bi - qi * br
        term_real = pr * br + pi * bi
        term_imag = pr * bi - pi * br
        object_keep[s] += jnp.where(first, term_real, term_imag)
        object_send[s] += jnp.where(first, term_imag, term_real)
    sum_real *= scale
    sum_imag *= scale
    probe_keep[...] = jnp.where(low, sum_real, sum_imag)
    probe_send[...] = jnp.where(low, sum_imag, sum_real)


def backward(info, probes, mine, other, amplitudes, power, power_other, spectrum, left, right, scale):
    modes, _, size, _ = probes.shape
    slots = mine.shape[0]
    plane = pl.BlockSpec((None, size, size), lambda m, info: (m, 0, 0))
    return pl.pallas_call(
        functools.partial(backward_kernel, size, slots, scale),
        grid_spec=pltpu.PrefetchScalarGridSpec(
            num_scalar_prefetch=1,
            grid=(modes,),
            in_specs=[
                pl.BlockSpec((None, 2, size, size), lambda m, info: (m, 0, 0, 0)),
                whole(mine.shape),
                whole(other.shape),
                whole(mine.shape),
                whole(power.shape),
                whole(power.shape),
                pl.BlockSpec((None, slots, size, 2 * size), lambda m, info: (m, 0, 0, 0)),
                whole(left.shape),
                whole(right.shape),
            ],
            out_specs=[plane, plane, whole(mine.shape), whole(mine.shape)],
            scratch_shapes=[pltpu.VMEM(mine.shape, f32)],
        ),
        out_shape=[jax.ShapeDtypeStruct((modes, size, size), f32)] * 2
        + [jax.ShapeDtypeStruct(mine.shape, f32)] * 2,
        compiler_params=params(),
        name="backward",
    )(info, probes, mine, other, amplitudes, power, power_other, spectrum, left, right)


def place_kernel(size, margin, tile, slots, groups, info, mine, other, columns, strips, frame):
    span = tile + 2 * margin
    frame[...] = jnp.zeros_like(frame)
    rows, cols = size + SUBLANES, size + LANES
    for slot in range(slots):
        base_row, base_col, row, col = window_of((info[2 * slot], info[2 * slot + 1]))
        patch = mine[slot] + other[slot]
        window = jnp.concatenate([patch, jnp.zeros((SUBLANES, size), f32)], axis=0)
        window = pltpu.roll(window, row, 0)
        window = jnp.concatenate([window, jnp.zeros((rows, LANES), f32)], axis=1)
        window = pltpu.roll(window, col, 1)
        at = (pl.ds(base_row, rows), pl.ds(base_col, cols))
        frame[at] = frame[at] + window
    columns[...] = frame[0:span, margin : margin + tile]
    for g in range(groups):
        start = pl.multiple_of(info[2 * slots + g], LANES)
        strips[g] = frame[0:span, pl.ds(start, margin)]


def place(info, mine, other, tile, groups):
    slots, size, _ = mine.shape
    margin = size // 2
    span = tile + 2 * margin
    return pl.pallas_call(
        functools.partial(place_kernel, size, margin, tile, slots, groups),
        grid_spec=pltpu.PrefetchScalarGridSpec(
            num_scalar_prefetch=1,
            grid=(1,),
            in_specs=[whole(mine.shape), whole(other.shape)],
            out_specs=[whole((span, tile)), whole((groups, span, margin))],
            scratch_shapes=[pltpu.VMEM((span + SUBLANES, span + LANES), f32)],
        ),
        out_shape=[
            jax.ShapeDtypeStruct((span, tile), f32),
            jax.ShapeDtypeStruct((groups, span, margin), f32),
        ],
        compiler_params=params(),
        name="place",
    )(info, mine, other)


def merge_kernel(margin, tile, groups, info, columns, *refs):
    arrived, (top, middle, bottom) = refs[:groups], refs[groups:]
    top[...] = columns[0:margin]
    middle[...] = columns[margin : margin + tile]
    bottom[...] = columns[margin + tile :]
    for g in range(groups):
        at = pl.ds(pl.multiple_of(info[g], LANES), margin)
        top[:, at] = top[:, at] + arrived[g][0:margin]
        middle[:, at] = middle[:, at] + arrived[g][margin : margin + tile]
        bottom[:, at] = bottom[:, at] + arrived[g][margin + tile :]


def merge(info, columns, arrived):
    span, tile = columns.shape
    margin = (span - tile) // 2
    shapes = [(margin, tile), (tile, tile), (margin, tile)]
    return pl.pallas_call(
        functools.partial(merge_kernel, margin, tile, len(arrived)),
        grid_spec=pltpu.PrefetchScalarGridSpec(
            num_scalar_prefetch=1,
            grid=(1,),
            in_specs=[whole(columns.shape)] + [whole(a.shape) for a in arrived],
            out_specs=[whole(s) for s in shapes],
        ),
        out_shape=[jax.ShapeDtypeStruct(s, f32) for s in shapes],
        compiler_params=params(),
        name="merge",
    )(info, columns, *arrived)


def finish_kernel(margin, tile, middle, above, below, out):
    out[0, 0:margin] = middle[0:margin] + above[...]
    out[0, margin : tile - margin] = middle[margin : tile - margin]
    out[0, tile - margin :] = middle[tile - margin :] + below[...]


def finish(middle, above, below):
    tile = middle.shape[0]
    margin = above.shape[0]
    return pl.pallas_call(
        functools.partial(finish_kernel, margin, tile),
        out_shape=jax.ShapeDtypeStruct((1, tile, tile), f32),
        compiler_params=params(),
        name="finish",
    )(middle, above, below)


def pairs(axis, bit):
    return [(i, i ^ (1 << bit)) for i in range(lax.axis_size(axis))]


def swap(value, dim):
    axis, bit = dim
    return lax.ppermute(value, axis, pairs(axis, bit))


def side_of(dim):
    axis, bit = dim
    return (lax.axis_index(axis) >> bit) & 1


def halves(value, side):
    count = value.shape[0] // 2
    keep = lax.dynamic_slice_in_dim(value, side * count, count, 0)
    send = lax.dynamic_slice_in_dim(value, (1 - side) * count, count, 0)
    return keep, send


def joined(mine, back, side):
    low = jnp.where(side == 0, mine, back)
    high = jnp.where(side == 0, back, mine)
    return jnp.concatenate([low, high], axis=0)


def total(value, dims):
    if not dims:
        return value
    if len(dims) == 1:
        return value + swap(value, dims[0])
    side = side_of(dims[0])
    keep, send = halves(value, side)
    mine = total(keep + swap(send, dims[0]), dims[1:])
    return joined(mine, swap(mine, dims[0]), side)


def shards(object_field, probe_modes, amplitudes, positions, counts):
    modes, _, size, _ = probe_modes.shape
    margin = size // 2
    tile = object_field.shape[-1]
    slots = positions.shape[2]
    rows, cols = lax.axis_size("row"), lax.axis_size("col")
    row, col, core = lax.axis_index("row"), lax.axis_index("col"), lax.axis_index("mode")
    left, right = (jnp.asarray(t) for t in dft_blocks(size))
    offsets = positions[0, 0].reshape(-1)

    field = lax.dynamic_index_in_dim(object_field, core, 0, keepdims=False)
    downward = [(i, i + 1) for i in range(rows - 1)]
    upward = [(i + 1, i) for i in range(rows - 1)]
    from_above = lax.ppermute(field[tile - margin :], "row", downward)
    from_below = lax.ppermute(field[:margin], "row", upward)
    if cols == 2:
        shifts = [[(0, 1), (1, 0)]]
        starts = [jnp.where(col == 0, tile - margin, 0)]
    else:
        shifts = [[(i, i + 1) for i in range(cols - 1)], [(i + 1, i) for i in range(cols - 1)]]
        starts = [jnp.int32(tile - margin), jnp.int32(0)]
    sides, uppers, lowers = [], [], []
    for shift, start in zip(shifts, starts):
        edge = lax.dynamic_slice(field, (0, start), (tile, margin))
        sides.append(lax.ppermute(edge, "col", shift))
        both = ("row", "col")
        uppers.append(
            lax.ppermute(
                edge[tile - margin :], both, [(a * cols + c, b * cols + d) for a, b in downward for c, d in shift]
            )
        )
        lowers.append(
            lax.ppermute(
                edge[:margin], both, [(a * cols + c, b * cols + d) for a, b in upward for c, d in shift]
            )
        )
    strips = [
        from_above, from_below, sides[0], sides[-1], uppers[0], uppers[-1], lowers[0], lowers[-1],
    ]
    flags = jnp.stack([core, (col > 0).astype(jnp.int32), (col < cols - 1).astype(jnp.int32)])
    mine = cut_patches(jnp.concatenate([flags, offsets]), object_field, strips, size, slots)
    core_dim = ("mode", 0)
    other = swap(mine, core_dim)

    spectrum, power = forward(core[None], probe_modes, mine, other, left, right)
    power_other = swap(power, core_dim)
    dims = [("col", b) for b in range(cols.bit_length() - 1)] + [
        ("row", b) for b in range(rows.bit_length() - 1)
    ]
    side = side_of(dims[0])
    probe_keep, probe_send, object_keep, object_send = backward(
        jnp.stack([core, side, counts[0, 0]]), probe_modes, mine, other, amplitudes[0, 0], power, power_other,
        spectrum, left, right, 1.0 / math.sqrt(rows * cols),
    )

    planes = []
    for m in range(modes):
        part = total(probe_keep[m] + swap(probe_send[m], dims[0]), dims[1:])
        planes.append(joined(part[None], swap(part, dims[0])[None], side))
    probe_grad = jnp.stack(planes)

    object_other = swap(object_send, core_dim)
    if cols == 2:
        out_starts = [jnp.where(col == 0, tile + margin, 0)]
        in_starts = [jnp.where(col == 0, tile - margin, 0)]
    else:
        out_starts = [jnp.int32(tile + margin), jnp.int32(0)]
        in_starts = [jnp.int32(0), jnp.int32(tile - margin)]
    columns, outgoing = place(
        jnp.concatenate([offsets, jnp.stack(out_starts)]), object_keep, object_other, tile, len(shifts)
    )
    arrived = [lax.ppermute(outgoing[g], "col", shift) for g, shift in enumerate(shifts)]
    top, middle, bottom = merge(jnp.stack(in_starts), columns, arrived)
    below = lax.ppermute(top, "row", upward)
    above = lax.ppermute(bottom, "row", downward)
    object_grad = finish(middle, above, below)
    return (object_grad, probe_grad)


def solution(mesh):
    return jax.shard_map(
        shards,
        mesh=mesh,
        in_specs=(
            P("scene", "row", "col"),
            P(("scene", "mode"), None, None, None),
            P(("scene", "row"), "col", None, None, None),
            P(("scene", "row"), "col", None, None),
            P(("scene", "row"), "col"),
        ),
        out_specs=(P(("scene", "mode"), "row", "col"), P(("scene", "mode"), None, None, None)),
        check_vma=False,
    )
```

```python
import functools
import math

import jax
import jax.numpy as jnp
import numpy as np
from jax import lax
from jax.experimental import pallas as pl
from jax.experimental.pallas import tpu as pltpu
from jax.sharding import PartitionSpec as P

damping = 0.1
LANES = 128
SUBLANES = 8
MIB = 1024 * 1024

CHUNKS = (("C", (0,)), ("A", (1,)), ("A", (2,)), ("A", (3,)))
ORDER = "0123410142321032140234023103"

f32 = jnp.float32
bf16 = jnp.bfloat16


def dft_blocks(size):
    index = np.arange(size, dtype=np.int64)
    angles = 2.0 * np.pi / size * (index[:, None] * index[None, :] % size)
    real = (np.cos(angles) / np.sqrt(size)).astype(np.float32).astype(bf16)
    imag = (-np.sin(angles) / np.sqrt(size)).astype(np.float32).astype(bf16)
    left = np.block([[real, -imag], [imag, real]])
    return left, np.ascontiguousarray(left.T)


def params(mebibytes):
    return pltpu.CompilerParams(vmem_limit_bytes=mebibytes * MIB)


def whole(shape):
    return pl.BlockSpec(shape, lambda *_: (0,) * len(shape))


ANYWHERE = pl.BlockSpec(memory_space=pl.ANY)
RESIDENT = pl.BlockSpec(memory_space=pltpu.VMEM)


def resident(value):
    return pltpu.with_memory_space_constraint(value, pltpu.VMEM)


def in_hbm(value):
    return pltpu.with_memory_space_constraint(value, pltpu.HBM)


def copies(sems):
    taken = iter(range(sems.shape[0]))

    def start(source, target):
        copy = pltpu.make_async_copy(source, target, sems.at[next(taken)])
        copy.start()
        return copy

    return start


def window_of(offset):
    base_row = pl.multiple_of(offset[0] // SUBLANES * SUBLANES, SUBLANES)
    base_col = pl.multiple_of(offset[1] // LANES * LANES, LANES)
    return base_row, base_col, offset[0] - base_row, offset[1] - base_col


def edges_kernel(margin, tile, groups, field, *refs):
    outs, sems = refs[:-1], refs[-1]
    start = copies(sems)
    own = field.at[lax.axis_index("mode")]
    moves = []
    for g in range(groups):
        if groups == 1:
            column = jnp.where(lax.axis_index("col") == 0, tile - margin, 0)
        else:
            column = (tile - margin, 0)[g]
        at = pl.ds(pl.multiple_of(column, LANES), margin)
        moves.append(start(own.at[:, at], outs[2 + g]))
    moves.append(start(own.at[pl.ds(0, margin)], outs[0]))
    moves.append(start(own.at[pl.ds(tile - margin, margin)], outs[1]))
    for move in moves:
        move.wait()


def edges(field, margin, groups):
    tile = field.shape[-1]
    shapes = [(margin, tile)] * 2 + [(tile, margin)] * groups
    return pl.pallas_call(
        functools.partial(edges_kernel, margin, tile, groups),
        in_specs=[ANYWHERE],
        out_specs=[RESIDENT] * len(shapes),
        out_shape=[pltpu.VMEM(s, f32) for s in shapes],
        scratch_shapes=[pltpu.SemaphoreType.DMA((len(shapes),))],
        compiler_params=params(1),
        name="edges",
    )(in_hbm(field))


def cut_kernel(
    size, margin, tile, slots, offsets, field, up, down, left, right, corners_left, corners_right, out, frame, sems
):
    start = copies(sems)
    low, high = pl.ds(0, margin), pl.ds(margin + tile, margin)
    mid = pl.ds(margin, tile)
    col = lax.axis_index("col")
    moves = [
        start(field.at[lax.axis_index("mode")], frame.at[mid, mid]),
        start(up, frame.at[low, mid]),
        start(down, frame.at[high, mid]),
        start(left, frame.at[mid, low]),
        start(right, frame.at[mid, high]),
        start(corners_left.at[0], frame.at[low, low]),
        start(corners_right.at[0], frame.at[low, high]),
        start(corners_left.at[1], frame.at[high, low]),
        start(corners_right.at[1], frame.at[high, high]),
    ]
    for move in moves:
        move.wait()
    span = tile + 2 * margin

    @pl.when(col == 0)
    def _():
        frame[0:span, 0:margin] = jnp.zeros((span, margin), f32)

    @pl.when(col == lax.axis_size("col") - 1)
    def _():
        frame[0:span, margin + tile : span] = jnp.zeros((span, margin), f32)

    rows, cols = size + SUBLANES, size + LANES
    for slot in range(slots):
        base_row, base_col, row, col = window_of((offsets[2 * slot], offsets[2 * slot + 1]))
        window = frame[pl.ds(base_row, rows), pl.ds(base_col, cols)]
        window = pltpu.roll(window, rows - row, 0)[:size]
        window = pltpu.roll(window, cols - col, 1)[:, :size]
        out[slot] = window


SMEM = pl.BlockSpec(memory_space=pltpu.SMEM)


def cut_patches(offsets, field, strips, size, slots):
    tile = field.shape[-1]
    margin = size // 2
    span = tile + 2 * margin
    return pl.pallas_call(
        functools.partial(cut_kernel, size, margin, tile, slots),
        in_specs=[SMEM, ANYWHERE] + [RESIDENT] * len(strips),
        out_specs=RESIDENT,
        out_shape=pltpu.VMEM((slots, size, size), f32),
        scratch_shapes=[
            pltpu.VMEM((span + SUBLANES, span + LANES), f32),
            pltpu.SemaphoreType.DMA((3 + len(strips),)),
        ],
        compiler_params=params(4),
        name="cut",
    )(offsets, in_hbm(field), *map(resident, strips))


def as_slot_rows(wave, size, slots):
    return jnp.concatenate(
        [
            jnp.concatenate(
                [wave[c * size : (c + 1) * size, s * size : (s + 1) * size] for c in range(2)], axis=1
            )
            for s in range(slots)
        ],
        axis=0,
    )


def staged(value):
    def kernel(source, target, sem):
        copy = pltpu.make_async_copy(source, target, sem)
        copy.start()
        copy.wait()

    return pl.pallas_call(
        kernel,
        in_specs=[ANYWHERE],
        out_specs=RESIDENT,
        out_shape=pltpu.VMEM(value.shape, value.dtype),
        scratch_shapes=[pltpu.SemaphoreType.DMA],
        compiler_params=params(1),
        name="stage",
    )(in_hbm(value))


def forward_kernel(size, slots, modes, mine, other, probes, tables, spectrum, power, spectrum_v, sems):
    start = copies(sems)
    leaving = []
    first = lax.axis_index("mode") == 0
    for m in range(modes):
        pr, pi = probes[m, 0], probes[m, 1]
        real, imag = [], []
        for s in range(slots):
            a, b = mine[s], other[s]
            qr, qi = jnp.where(first, a, b), jnp.where(first, b, a)
            real.append((pr * qr - pi * qi).astype(bf16))
            imag.append((pr * qi + pi * qr).astype(bf16))
        wave = jnp.concatenate([jnp.concatenate(real, axis=1), jnp.concatenate(imag, axis=1)], axis=0)
        half = jnp.dot(tables[0], wave, preferred_element_type=f32).astype(bf16)
        full = jnp.dot(as_slot_rows(half, size, slots), tables[1], preferred_element_type=f32)
        for s in range(slots):
            rows = full[s * size : (s + 1) * size]
            spectrum_v[m, s] = rows
            square = rows[:, :size] * rows[:, :size] + rows[:, size:] * rows[:, size:]
            power[s] = square if m == 0 else power[s] + square
        leaving.append(start(spectrum_v.at[m], spectrum.at[m]))
    for move in leaving:
        move.wait()


def forward(probes, mine, other, tables):
    modes, _, size, _ = probes.shape
    slots = mine.shape[0]
    spectra = (modes, slots, size, 2 * size)
    return pl.pallas_call(
        functools.partial(forward_kernel, size, slots, modes),
        in_specs=[RESIDENT] * 4,
        out_specs=[ANYWHERE, RESIDENT],
        out_shape=[pltpu.HBM(spectra, f32), pltpu.VMEM(mine.shape, f32)],
        scratch_shapes=[
            pltpu.VMEM(spectra, f32),
            pltpu.SemaphoreType.DMA((modes,)),
        ],
        compiler_params=params(8),
        name="forward",
    )(*map(resident, (mine, other, probes, tables)))


def backward_kernel(
    size, slots, chunks, scale, live, spectrum, amplitudes, tables, power, power_other, probes, mine, other, *refs
):
    outs, (spectrum_v, amplitudes_v, tables_v, planes_v, objects_v, weight, sems) = refs[:-7], refs[-7:]
    modes = probes.shape[0]
    start = copies(sems)
    fetched = start(amplitudes, amplitudes_v)
    arriving = [start(spectrum.at[0], spectrum_v.at[0])]
    needed = [start(tables.at[j], tables_v.at[j]) for j in (1, 0)]
    arriving += [start(spectrum.at[m], spectrum_v.at[m]) for m in range(1, modes)]
    leaving = []
    first = lax.axis_index("mode") == 0
    places = {m: (c, k) for c, chunk in enumerate(chunks) for k, m in enumerate(chunk)}
    fetched.wait()
    for s in range(slots):
        active = (s < live[0]).astype(f32)
        total = power[s] + power_other[s]
        weight[s] = active * (1.0 - amplitudes_v[s] / jnp.sqrt(total + damping))
    for m in range(modes):
        arriving[m].wait()
        real, imag = [], []
        for s in range(slots):
            w = weight[s]
            real.append((w * spectrum_v[m, s, :, :size]).astype(bf16))
            imag.append((w * spectrum_v[m, s, :, size:]).astype(bf16))
        hat = jnp.concatenate([jnp.concatenate(real, axis=1), jnp.concatenate(imag, axis=1)], axis=0)
        if m == 0:
            for move in needed:
                move.wait()
        half = jnp.dot(tables_v[1], hat, preferred_element_type=f32).astype(bf16)
        back = jnp.dot(as_slot_rows(half, size, slots), tables_v[0], preferred_element_type=f32)
        pr, pi = probes[m, 0], probes[m, 1]
        sum_real = sum_imag = None
        for s in range(slots):
            br = back[s * size : (s + 1) * size, :size]
            bi = back[s * size : (s + 1) * size, size:]
            a, b = mine[s], other[s]
            qr, qi = jnp.where(first, a, b), jnp.where(first, b, a)
            add_real, add_imag = qr * br + qi * bi, qr * bi - qi * br
            sum_real = add_real if s == 0 else sum_real + add_real
            sum_imag = add_imag if s == 0 else sum_imag + add_imag
            term_real = pr * br + pi * bi
            term_imag = pr * bi - pi * br
            terms = jnp.where(first, term_real, term_imag), jnp.where(first, term_imag, term_real)
            for j, term in enumerate(terms):
                objects_v[j, s] = term if m == 0 else objects_v[j, s] + term
        sum_real, sum_imag = sum_real * scale, sum_imag * scale
        if m > 1:
            for _ in range(2):
                leaving.pop(0).wait()
        c, k = places[m]
        low = live[1 + c] == 0
        planes_v[m % 2, 0] = jnp.where(low, sum_real, sum_imag)
        planes_v[m % 2, 1] = jnp.where(low, sum_imag, sum_real)
        rows = pl.ds(k * size, size)
        leaving += [start(planes_v.at[m % 2, j], outs[2 * c + j].at[rows]) for j in range(2)]
    leaving += [start(objects_v.at[j], outs[2 * len(chunks) + j]) for j in range(2)]
    for move in leaving:
        move.wait()


def backward(live, chunks, probes, mine, other, amplitudes, power, power_other, spectrum, tables, scale):
    modes, _, size, _ = probes.shape
    slots = mine.shape[0]
    operands = [power, power_other, probes, mine, other]
    planes = [pltpu.HBM((len(chunk) * size, size), f32) for chunk in chunks for _ in range(2)]
    return pl.pallas_call(
        functools.partial(backward_kernel, size, slots, chunks, scale),
        in_specs=[SMEM] + [ANYWHERE] * 3 + [RESIDENT] * len(operands),
        out_specs=[ANYWHERE] * (len(planes) + 2),
        out_shape=planes + [pltpu.HBM(mine.shape, f32)] * 2,
        scratch_shapes=[
            pltpu.VMEM(spectrum.shape, f32),
            pltpu.VMEM(mine.shape, f32),
            pltpu.VMEM(tables.shape, bf16),
            pltpu.VMEM((2, 2, size, size), f32),
            pltpu.VMEM((2,) + mine.shape, f32),
            pltpu.VMEM(mine.shape, f32),
            pltpu.SemaphoreType.DMA((3 * modes + 5,)),
        ],
        compiler_params=params(12),
        name="backward",
    )(live, *map(in_hbm, (spectrum, amplitudes, tables)), *map(resident, operands))


def place_kernel(size, margin, tile, slots, groups, info, mine, other, columns, strips, frame):
    span = tile + 2 * margin
    frame[...] = jnp.zeros_like(frame)
    rows, cols = size + SUBLANES, size + LANES
    for slot in range(slots):
        base_row, base_col, row, col = window_of((info[2 * slot], info[2 * slot + 1]))
        patch = mine[slot] + other[slot]
        window = jnp.concatenate([patch, jnp.zeros((SUBLANES, size), f32)], axis=0)
        window = pltpu.roll(window, row, 0)
        window = jnp.concatenate([window, jnp.zeros((rows, LANES), f32)], axis=1)
        window = pltpu.roll(window, col, 1)
        at = (pl.ds(base_row, rows), pl.ds(base_col, cols))
        frame[at] = frame[at] + window
    columns[...] = frame[0:span, margin : margin + tile]
    for g in range(groups):
        start = pl.multiple_of(info[2 * slots + g], LANES)
        strips[g] = frame[0:span, pl.ds(start, margin)]


def place(info, mine, other, tile, groups):
    slots, size, _ = mine.shape
    margin = size // 2
    span = tile + 2 * margin
    return pl.pallas_call(
        functools.partial(place_kernel, size, margin, tile, slots, groups),
        grid_spec=pltpu.PrefetchScalarGridSpec(
            num_scalar_prefetch=1,
            grid=(1,),
            in_specs=[whole(mine.shape), whole(other.shape)],
            out_specs=[whole((span, tile)), whole((groups, span, margin))],
            scratch_shapes=[pltpu.VMEM((span + SUBLANES, span + LANES), f32)],
        ),
        out_shape=[
            jax.ShapeDtypeStruct((span, tile), f32),
            jax.ShapeDtypeStruct((groups, span, margin), f32),
        ],
        compiler_params=params(5),
        name="place",
    )(info, mine, other)


def merge_kernel(margin, tile, groups, info, columns, *refs):
    arrived, (top, middle, bottom) = refs[:groups], refs[groups:]
    top[...] = columns[0:margin]
    middle[...] = columns[margin : margin + tile]
    bottom[...] = columns[margin + tile :]
    for g in range(groups):
        at = pl.ds(pl.multiple_of(info[g], LANES), margin)
        top[:, at] = top[:, at] + arrived[g][0:margin]
        middle[:, at] = middle[:, at] + arrived[g][margin : margin + tile]
        bottom[:, at] = bottom[:, at] + arrived[g][margin + tile :]


def merge(info, columns, arrived):
    span, tile = columns.shape
    margin = (span - tile) // 2
    shapes = [(margin, tile), (tile, tile), (margin, tile)]
    return pl.pallas_call(
        functools.partial(merge_kernel, margin, tile, len(arrived)),
        grid_spec=pltpu.PrefetchScalarGridSpec(
            num_scalar_prefetch=1,
            grid=(1,),
            in_specs=[whole(columns.shape)] + [whole(a.shape) for a in arrived],
            out_specs=[whole(s) for s in shapes],
        ),
        out_shape=[jax.ShapeDtypeStruct(s, f32) for s in shapes],
        compiler_params=params(2),
        name="merge",
    )(info, columns, *arrived)


def finish_kernel(margin, tile, middle, above, below, out):
    out[0, 0:margin] = middle[0:margin] + above[...]
    out[0, margin : tile - margin] = middle[margin : tile - margin]
    out[0, tile - margin :] = middle[tile - margin :] + below[...]


def finish(middle, above, below):
    tile = middle.shape[0]
    margin = above.shape[0]
    return pl.pallas_call(
        functools.partial(finish_kernel, margin, tile),
        out_shape=jax.ShapeDtypeStruct((1, tile, tile), f32),
        compiler_params=params(2),
        name="finish",
    )(middle, above, below)


AXES = ("row", "col", "mode")


def crossed(turn):
    sizes = [lax.axis_size(axis) for axis in AXES]
    perm = []
    for index in np.ndindex(*sizes):
        axis, bit = turn[index[2] % 2]
        partner = list(index)
        partner[AXES.index(axis)] ^= 1 << bit
        perm.append(tuple(int(np.ravel_multi_index(i, sizes)) for i in (index, partner)))
    sides = [(lax.axis_index(axis) >> bit) & 1 for axis, bit in turn]
    return perm, jnp.where(lax.axis_index("mode") == 0, sides[0], sides[1])


def swap(value, turn):
    return lax.ppermute(value, AXES, crossed(turn)[0])


def halves(value, side):
    count = value.shape[0] // 2
    keep = lax.dynamic_slice_in_dim(value, side * count, count, 0)
    send = lax.dynamic_slice_in_dim(value, (1 - side) * count, count, 0)
    return keep, send


def joined(mine, back, side):
    low = jnp.where(side == 0, mine, back)
    high = jnp.where(side == 0, back, mine)
    return jnp.concatenate([low, high], axis=0)


def summed(keep, send, turns):
    sides = [crossed(turn)[1] for turn in turns]
    send = yield send
    got = yield swap(send, turns[0])
    value = keep + got
    for turn, side in zip(turns[1:-1], sides[1:-1]):
        keep, send = halves(value, side)
        got = yield swap(send, turn)
        value = keep + got
    got = yield swap(value, turns[-1])
    value = value + got
    for turn, side in reversed(list(zip(turns[1:-1], sides[1:-1]))):
        back = yield swap(value, turn)
        value = joined(value, back, side)
    back = yield swap(value, turns[0])
    return (value, back)


def woven(jobs, order):
    waiting = [next(job) for job in jobs]
    results = [None] * len(jobs)
    token = None
    for j in order:
        got = waiting[j]
        if token is not None:
            got, _ = lax.optimization_barrier((got, token))
        try:
            waiting[j] = jobs[j].send(got)
            token = got
        except StopIteration as stop:
            results[j] = stop.value
            token = got
    return results


def order_of(lengths):
    order = [int(c) for c in ORDER]
    if [order.count(j) for j in range(len(lengths))] == lengths:
        return order
    steps = [(k + (j if j < len(lengths) - 1 else 1.5), j) for j, n in enumerate(lengths) for k in range(n)]
    return [j for _, j in sorted(steps)]


def shards(object_field, probe_modes, amplitudes, positions, counts):
    modes, _, size, _ = probe_modes.shape
    margin = size // 2
    tile = object_field.shape[-1]
    slots = positions.shape[2]
    rows, cols = lax.axis_size("row"), lax.axis_size("col")
    row, col, core = lax.axis_index("row"), lax.axis_index("col"), lax.axis_index("mode")
    tables = jnp.asarray(np.stack(dft_blocks(size)))
    offsets = positions[0, 0].reshape(-1)

    downward = [(i, i + 1) for i in range(rows - 1)]
    upward = [(i + 1, i) for i in range(rows - 1)]
    if cols == 2:
        shifts = [[(0, 1), (1, 0)]]
    else:
        shifts = [[(i, i + 1) for i in range(cols - 1)], [(i + 1, i) for i in range(cols - 1)]]
    top, bottom, *rest = edges(object_field, margin, len(shifts))
    from_above = lax.ppermute(bottom, "row", downward)
    from_below = lax.ppermute(top, "row", upward)
    sides, corners = [], []
    for g, shift in enumerate(shifts):
        sides.append(lax.ppermute(rest[g], "col", shift))
        at = jnp.where(col == 0, tile - margin, 0) if cols == 2 else (tile - margin, 0)[g]
        ends = [lax.dynamic_slice_in_dim(strip, at, margin, 1) for strip in (from_above, from_below)]
        corners.append(lax.ppermute(jnp.stack(ends), "col", shift))
    strips = [from_above, from_below, sides[0], sides[-1], corners[0], corners[-1]]
    mine = cut_patches(offsets, object_field, strips, size, slots)
    sibling = [("mode", 0)] * 2
    other = swap(mine, sibling)

    spectrum, power = forward(probe_modes, mine, other, staged(tables))
    power_other = swap(power, sibling)
    col_dims = [("col", b) for b in range(cols.bit_length() - 1)]
    row_dims = [("row", b) for b in range(rows.bit_length() - 1)]
    x, z = col_dims[0], row_dims[0]
    rest = [(dim, dim) for dim in col_dims[1:] + row_dims[1:]]
    turns = {"A": [(x, x), (z, z)] + rest, "C": [(z, z), (x, x)] + rest, "S": [(x, z), (z, x)] + rest}
    plans = [turns[kind] for kind, _ in CHUNKS]
    sides = [crossed(plan[0])[1] for plan in plans]
    *planes, object_keep, object_send = backward(
        jnp.stack([counts[0, 0]] + sides), [chunk for _, chunk in CHUNKS], probe_modes, mine, other,
        amplitudes[0, 0], power, power_other, spectrum, tables, 1.0 / math.sqrt(rows * cols),
    )

    def folded():
        if cols == 2:
            out_starts = [jnp.where(col == 0, tile + margin, 0)]
            in_starts = [jnp.where(col == 0, tile - margin, 0)]
        else:
            out_starts = [jnp.int32(tile + margin), jnp.int32(0)]
            in_starts = [jnp.int32(0), jnp.int32(tile - margin)]
        sent = yield object_send
        object_other = yield swap(sent, sibling)
        columns, outgoing = place(
            jnp.concatenate([offsets, jnp.stack(out_starts)]), object_keep, object_other, tile, len(shifts)
        )
        arrived = yield [lax.ppermute(outgoing[g], "col", shift) for g, shift in enumerate(shifts)]
        top, middle, bottom = merge(jnp.stack(in_starts), columns, arrived)
        above, below = yield (lax.ppermute(bottom, "row", downward), lax.ppermute(top, "row", upward))
        return finish(middle, above, below)

    jobs = [summed(*parts) for parts in zip(planes[0::2], planes[1::2], plans)] + [folded()]
    lengths = [2 * len(plan) for plan in plans] + [4]
    *sums, object_grad = woven(jobs, order_of(lengths))
    grads = {}
    for (own, back), side, (_, chunk) in zip(sums, sides, CHUNKS):
        low, high = jnp.where(side == 0, own, back), jnp.where(side == 0, back, own)
        for k, m in enumerate(chunk):
            grads[m] = jnp.stack([part[k * size : (k + 1) * size] for part in (low, high)])
    probe_grad = jnp.stack([grads[m] for m in range(modes)])
    return (object_grad, probe_grad)


def solution(mesh):
    return jax.shard_map(
        shards,
        mesh=mesh,
        in_specs=(
            P("scene", "row", "col"),
            P(("scene", "mode"), None, None, None),
            P(("scene", "row"), "col", None, None, None),
            P(("scene", "row"), "col", None, None),
            P(("scene", "row"), "col"),
        ),
        out_specs=(P(("scene", "mode"), "row", "col"), P(("scene", "mode"), None, None, None)),
        check_vma=False,
    )
```

```python
import functools
import math

import jax
import jax.numpy as jnp
import numpy as np
from jax import lax
from jax.experimental import pallas as pl
from jax.experimental.pallas import tpu as pltpu
from jax.sharding import PartitionSpec as P

damping = 0.1
LANES = 128
SUBLANES = 8
MIB = 1024 * 1024

CHUNKS = (("C", (0,)), ("A", (1,)), ("S", (2, 3)))

f32 = jnp.float32
bf16 = jnp.bfloat16


def dft_blocks(size):
    index = np.arange(size, dtype=np.int64)
    angles = 2.0 * np.pi / size * (index[:, None] * index[None, :] % size)
    real = (np.cos(angles) / np.sqrt(size)).astype(np.float32).astype(bf16)
    imag = (-np.sin(angles) / np.sqrt(size)).astype(np.float32).astype(bf16)
    left = np.block([[real, -imag], [imag, real]])
    return left, np.ascontiguousarray(left.T)


def params(mebibytes):
    return pltpu.CompilerParams(vmem_limit_bytes=mebibytes * MIB)


def whole(shape):
    return pl.BlockSpec(shape, lambda *_: (0,) * len(shape))


ANYWHERE = pl.BlockSpec(memory_space=pl.ANY)
RESIDENT = pl.BlockSpec(memory_space=pltpu.VMEM)


def resident(value):
    return pltpu.with_memory_space_constraint(value, pltpu.VMEM)


def in_hbm(value):
    return pltpu.with_memory_space_constraint(value, pltpu.HBM)


def copies(sems):
    taken = iter(range(sems.shape[0]))

    def start(source, target):
        copy = pltpu.make_async_copy(source, target, sems.at[next(taken)])
        copy.start()
        return copy

    return start


def window_of(offset):
    base_row = pl.multiple_of(offset[0] // SUBLANES * SUBLANES, SUBLANES)
    base_col = pl.multiple_of(offset[1] // LANES * LANES, LANES)
    return base_row, base_col, offset[0] - base_row, offset[1] - base_col


def edges_kernel(margin, tile, groups, field, *refs):
    outs, sems = refs[:-1], refs[-1]
    start = copies(sems)
    own = field.at[lax.axis_index("mode")]
    moves = []
    for g in range(groups):
        if groups == 1:
            column = jnp.where(lax.axis_index("col") == 0, tile - margin, 0)
        else:
            column = (tile - margin, 0)[g]
        at = pl.ds(pl.multiple_of(column, LANES), margin)
        moves.append(start(own.at[:, at], outs[2 + g]))
    moves.append(start(own.at[pl.ds(0, margin)], outs[0]))
    moves.append(start(own.at[pl.ds(tile - margin, margin)], outs[1]))
    for move in moves:
        move.wait()


def edges(field, margin, groups):
    tile = field.shape[-1]
    shapes = [(margin, tile)] * 2 + [(tile, margin)] * groups
    return pl.pallas_call(
        functools.partial(edges_kernel, margin, tile, groups),
        in_specs=[ANYWHERE],
        out_specs=[RESIDENT] * len(shapes),
        out_shape=[pltpu.VMEM(s, f32) for s in shapes],
        scratch_shapes=[pltpu.SemaphoreType.DMA((len(shapes),))],
        compiler_params=params(1),
        name="edges",
    )(in_hbm(field))


def cut_kernel(
    size, margin, tile, slots, offsets, field, up, down, left, right, corners_left, corners_right, out, frame, sems
):
    start = copies(sems)
    low, high = pl.ds(0, margin), pl.ds(margin + tile, margin)
    mid = pl.ds(margin, tile)
    col = lax.axis_index("col")
    moves = [
        start(field.at[lax.axis_index("mode")], frame.at[mid, mid]),
        start(up, frame.at[low, mid]),
        start(down, frame.at[high, mid]),
        start(left, frame.at[mid, low]),
        start(right, frame.at[mid, high]),
        start(corners_left.at[0], frame.at[low, low]),
        start(corners_right.at[0], frame.at[low, high]),
        start(corners_left.at[1], frame.at[high, low]),
        start(corners_right.at[1], frame.at[high, high]),
    ]
    for move in moves:
        move.wait()
    span = tile + 2 * margin

    @pl.when(col == 0)
    def _():
        frame[0:span, 0:margin] = jnp.zeros((span, margin), f32)

    @pl.when(col == lax.axis_size("col") - 1)
    def _():
        frame[0:span, margin + tile : span] = jnp.zeros((span, margin), f32)

    rows, cols = size + SUBLANES, size + LANES
    for slot in range(slots):
        base_row, base_col, row, col = window_of((offsets[2 * slot], offsets[2 * slot + 1]))
        window = frame[pl.ds(base_row, rows), pl.ds(base_col, cols)]
        window = pltpu.roll(window, rows - row, 0)[:size]
        window = pltpu.roll(window, cols - col, 1)[:, :size]
        out[slot] = window


SMEM = pl.BlockSpec(memory_space=pltpu.SMEM)


def cut_patches(offsets, field, strips, size, slots):
    tile = field.shape[-1]
    margin = size // 2
    span = tile + 2 * margin
    return pl.pallas_call(
        functools.partial(cut_kernel, size, margin, tile, slots),
        in_specs=[SMEM, ANYWHERE] + [RESIDENT] * len(strips),
        out_specs=RESIDENT,
        out_shape=pltpu.VMEM((slots, size, size), f32),
        scratch_shapes=[
            pltpu.VMEM((span + SUBLANES, span + LANES), f32),
            pltpu.SemaphoreType.DMA((3 + len(strips),)),
        ],
        compiler_params=params(4),
        name="cut",
    )(offsets, in_hbm(field), *map(resident, strips))


def as_slot_rows(wave, size, slots):
    return jnp.concatenate(
        [
            jnp.concatenate(
                [wave[c * size : (c + 1) * size, s * size : (s + 1) * size] for c in range(2)], axis=1
            )
            for s in range(slots)
        ],
        axis=0,
    )


def staged(value):
    def kernel(source, target, sem):
        copy = pltpu.make_async_copy(source, target, sem)
        copy.start()
        copy.wait()

    return pl.pallas_call(
        kernel,
        in_specs=[ANYWHERE],
        out_specs=RESIDENT,
        out_shape=pltpu.VMEM(value.shape, value.dtype),
        scratch_shapes=[pltpu.SemaphoreType.DMA],
        compiler_params=params(1),
        name="stage",
    )(in_hbm(value))


def forward_kernel(size, slots, modes, mine, other, probes, tables, spectrum, power, spectrum_v, sems):
    start = copies(sems)
    leaving = []
    first = lax.axis_index("mode") == 0
    for m in range(modes):
        pr, pi = probes[m, 0], probes[m, 1]
        real, imag = [], []
        for s in range(slots):
            a, b = mine[s], other[s]
            qr, qi = jnp.where(first, a, b), jnp.where(first, b, a)
            real.append((pr * qr - pi * qi).astype(bf16))
            imag.append((pr * qi + pi * qr).astype(bf16))
        wave = jnp.concatenate([jnp.concatenate(real, axis=1), jnp.concatenate(imag, axis=1)], axis=0)
        half = jnp.dot(tables[0], wave, preferred_element_type=f32).astype(bf16)
        full = jnp.dot(as_slot_rows(half, size, slots), tables[1], preferred_element_type=f32)
        for s in range(slots):
            rows = full[s * size : (s + 1) * size]
            spectrum_v[m, s] = rows
            square = rows[:, :size] * rows[:, :size] + rows[:, size:] * rows[:, size:]
            power[s] = square if m == 0 else power[s] + square
        leaving.append(start(spectrum_v.at[m], spectrum.at[m]))
    for move in leaving:
        move.wait()


def forward(probes, mine, other, tables):
    modes, _, size, _ = probes.shape
    slots = mine.shape[0]
    spectra = (modes, slots, size, 2 * size)
    return pl.pallas_call(
        functools.partial(forward_kernel, size, slots, modes),
        in_specs=[RESIDENT] * 4,
        out_specs=[ANYWHERE, RESIDENT],
        out_shape=[pltpu.HBM(spectra, f32), pltpu.VMEM(mine.shape, f32)],
        scratch_shapes=[
            pltpu.VMEM(spectra, f32),
            pltpu.SemaphoreType.DMA((modes,)),
        ],
        compiler_params=params(8),
        name="forward",
    )(*map(resident, (mine, other, probes, tables)))


def backward_kernel(
    size, slots, chunks, scale, live, spectrum, amplitudes, tables, power, power_other, probes, mine, other, *refs
):
    outs, (spectrum_v, amplitudes_v, tables_v, planes_v, objects_v, weight, sems) = refs[:-7], refs[-7:]
    modes = probes.shape[0]
    start = copies(sems)
    fetched = start(amplitudes, amplitudes_v)
    arriving = [start(spectrum.at[0], spectrum_v.at[0])]
    needed = [start(tables.at[j], tables_v.at[j]) for j in (1, 0)]
    arriving += [start(spectrum.at[m], spectrum_v.at[m]) for m in range(1, modes)]
    leaving = []
    first = lax.axis_index("mode") == 0
    places = {m: (c, k) for c, chunk in enumerate(chunks) for k, m in enumerate(chunk)}
    fetched.wait()
    for s in range(slots):
        active = (s < live[0]).astype(f32)
        total = power[s] + power_other[s]
        weight[s] = active * (1.0 - amplitudes_v[s] / jnp.sqrt(total + damping))
    for m in range(modes):
        arriving[m].wait()
        real, imag = [], []
        for s in range(slots):
            w = weight[s]
            real.append((w * spectrum_v[m, s, :, :size]).astype(bf16))
            imag.append((w * spectrum_v[m, s, :, size:]).astype(bf16))
        hat = jnp.concatenate([jnp.concatenate(real, axis=1), jnp.concatenate(imag, axis=1)], axis=0)
        if m == 0:
            for move in needed:
                move.wait()
        half = jnp.dot(tables_v[1], hat, preferred_element_type=f32).astype(bf16)
        back = jnp.dot(as_slot_rows(half, size, slots), tables_v[0], preferred_element_type=f32)
        pr, pi = probes[m, 0], probes[m, 1]
        sum_real = sum_imag = None
        for s in range(slots):
            br = back[s * size : (s + 1) * size, :size]
            bi = back[s * size : (s + 1) * size, size:]
            a, b = mine[s], other[s]
            qr, qi = jnp.where(first, a, b), jnp.where(first, b, a)
            add_real, add_imag = qr * br + qi * bi, qr * bi - qi * br
            sum_real = add_real if s == 0 else sum_real + add_real
            sum_imag = add_imag if s == 0 else sum_imag + add_imag
            term_real = pr * br + pi * bi
            term_imag = pr * bi - pi * br
            terms = jnp.where(first, term_real, term_imag), jnp.where(first, term_imag, term_real)
            for j, term in enumerate(terms):
                objects_v[j, s] = term if m == 0 else objects_v[j, s] + term
        sum_real, sum_imag = sum_real * scale, sum_imag * scale
        if m > 1:
            for _ in range(2):
                leaving.pop(0).wait()
        c, k = places[m]
        low = live[1 + c] == 0
        planes_v[m % 2, 0] = jnp.where(low, sum_real, sum_imag)
        planes_v[m % 2, 1] = jnp.where(low, sum_imag, sum_real)
        rows = pl.ds(k * size, size)
        leaving += [start(planes_v.at[m % 2, j], outs[2 * c + j].at[rows]) for j in range(2)]
    leaving += [start(objects_v.at[j], outs[2 * len(chunks) + j]) for j in range(2)]
    for move in leaving:
        move.wait()


def backward(live, chunks, probes, mine, other, amplitudes, power, power_other, spectrum, tables, scale):
    modes, _, size, _ = probes.shape
    slots = mine.shape[0]
    operands = [power, power_other, probes, mine, other]
    planes = [pltpu.HBM((len(chunk) * size, size), f32) for chunk in chunks for _ in range(2)]
    return pl.pallas_call(
        functools.partial(backward_kernel, size, slots, chunks, scale),
        in_specs=[SMEM] + [ANYWHERE] * 3 + [RESIDENT] * len(operands),
        out_specs=[ANYWHERE] * (len(planes) + 2),
        out_shape=planes + [pltpu.HBM(mine.shape, f32)] * 2,
        scratch_shapes=[
            pltpu.VMEM(spectrum.shape, f32),
            pltpu.VMEM(mine.shape, f32),
            pltpu.VMEM(tables.shape, bf16),
            pltpu.VMEM((2, 2, size, size), f32),
            pltpu.VMEM((2,) + mine.shape, f32),
            pltpu.VMEM(mine.shape, f32),
            pltpu.SemaphoreType.DMA((3 * modes + 5,)),
        ],
        compiler_params=params(12),
        name="backward",
    )(live, *map(in_hbm, (spectrum, amplitudes, tables)), *map(resident, operands))


def place_kernel(size, margin, tile, slots, groups, info, mine, other, columns, strips, frame):
    span = tile + 2 * margin
    frame[...] = jnp.zeros_like(frame)
    rows, cols = size + SUBLANES, size + LANES
    for slot in range(slots):
        base_row, base_col, row, col = window_of((info[2 * slot], info[2 * slot + 1]))
        patch = mine[slot] + other[slot]
        window = jnp.concatenate([patch, jnp.zeros((SUBLANES, size), f32)], axis=0)
        window = pltpu.roll(window, row, 0)
        window = jnp.concatenate([window, jnp.zeros((rows, LANES), f32)], axis=1)
        window = pltpu.roll(window, col, 1)
        at = (pl.ds(base_row, rows), pl.ds(base_col, cols))
        frame[at] = frame[at] + window
    columns[...] = frame[0:span, margin : margin + tile]
    for g in range(groups):
        start = pl.multiple_of(info[2 * slots + g], LANES)
        strips[g] = frame[0:span, pl.ds(start, margin)]


def place(info, mine, other, tile, groups):
    slots, size, _ = mine.shape
    margin = size // 2
    span = tile + 2 * margin
    return pl.pallas_call(
        functools.partial(place_kernel, size, margin, tile, slots, groups),
        grid_spec=pltpu.PrefetchScalarGridSpec(
            num_scalar_prefetch=1,
            grid=(1,),
            in_specs=[whole(mine.shape), whole(other.shape)],
            out_specs=[whole((span, tile)), whole((groups, span, margin))],
            scratch_shapes=[pltpu.VMEM((span + SUBLANES, span + LANES), f32)],
        ),
        out_shape=[
            jax.ShapeDtypeStruct((span, tile), f32),
            jax.ShapeDtypeStruct((groups, span, margin), f32),
        ],
        compiler_params=params(5),
        name="place",
    )(info, mine, other)


def merge_kernel(margin, tile, groups, info, columns, *refs):
    arrived, (top, middle, bottom) = refs[:groups], refs[groups:]
    top[...] = columns[0:margin]
    middle[...] = columns[margin : margin + tile]
    bottom[...] = columns[margin + tile :]
    for g in range(groups):
        at = pl.ds(pl.multiple_of(info[g], LANES), margin)
        top[:, at] = top[:, at] + arrived[g][0:margin]
        middle[:, at] = middle[:, at] + arrived[g][margin : margin + tile]
        bottom[:, at] = bottom[:, at] + arrived[g][margin + tile :]


def merge(info, columns, arrived):
    span, tile = columns.shape
    margin = (span - tile) // 2
    shapes = [(margin, tile), (tile, tile), (margin, tile)]
    return pl.pallas_call(
        functools.partial(merge_kernel, margin, tile, len(arrived)),
        grid_spec=pltpu.PrefetchScalarGridSpec(
            num_scalar_prefetch=1,
            grid=(1,),
            in_specs=[whole(columns.shape)] + [whole(a.shape) for a in arrived],
            out_specs=[whole(s) for s in shapes],
        ),
        out_shape=[jax.ShapeDtypeStruct(s, f32) for s in shapes],
        compiler_params=params(2),
        name="merge",
    )(info, columns, *arrived)


def finish_kernel(margin, tile, middle, above, below, out):
    out[0, 0:margin] = middle[0:margin] + above[...]
    out[0, margin : tile - margin] = middle[margin : tile - margin]
    out[0, tile - margin :] = middle[tile - margin :] + below[...]


def finish(middle, above, below):
    tile = middle.shape[0]
    margin = above.shape[0]
    return pl.pallas_call(
        functools.partial(finish_kernel, margin, tile),
        out_shape=jax.ShapeDtypeStruct((1, tile, tile), f32),
        compiler_params=params(2),
        name="finish",
    )(middle, above, below)


AXES = ("row", "col", "mode")


def crossed(turn):
    sizes = [lax.axis_size(axis) for axis in AXES]
    perm = []
    for index in np.ndindex(*sizes):
        axis, bit = turn[index[2] % 2]
        partner = list(index)
        partner[AXES.index(axis)] ^= 1 << bit
        perm.append(tuple(int(np.ravel_multi_index(i, sizes)) for i in (index, partner)))
    sides = [(lax.axis_index(axis) >> bit) & 1 for axis, bit in turn]
    return perm, jnp.where(lax.axis_index("mode") == 0, sides[0], sides[1])


def swap(value, turn):
    return lax.ppermute(value, AXES, crossed(turn)[0])


def halves(value, side):
    count = value.shape[0] // 2
    keep = lax.dynamic_slice_in_dim(value, side * count, count, 0)
    send = lax.dynamic_slice_in_dim(value, (1 - side) * count, count, 0)
    return keep, send


def joined(mine, back, side):
    low = jnp.where(side == 0, mine, back)
    high = jnp.where(side == 0, back, mine)
    return jnp.concatenate([low, high], axis=0)


def summed(keep, send, turns):
    sides = [crossed(turn)[1] for turn in turns]
    value = keep + swap(send, turns[0])
    for turn, side in zip(turns[1:-1], sides[1:-1]):
        keep, send = halves(value, side)
        value = keep + swap(send, turn)
    value = value + swap(value, turns[-1])
    for turn, side in reversed(list(zip(turns[1:-1], sides[1:-1]))):
        value = joined(value, swap(value, turn), side)
    return value, swap(value, turns[0])


def shards(object_field, probe_modes, amplitudes, positions, counts):
    modes, _, size, _ = probe_modes.shape
    margin = size // 2
    tile = object_field.shape[-1]
    slots = positions.shape[2]
    rows, cols = lax.axis_size("row"), lax.axis_size("col")
    row, col, core = lax.axis_index("row"), lax.axis_index("col"), lax.axis_index("mode")
    tables = jnp.asarray(np.stack(dft_blocks(size)))
    offsets = positions[0, 0].reshape(-1)

    downward = [(i, i + 1) for i in range(rows - 1)]
    upward = [(i + 1, i) for i in range(rows - 1)]
    if cols == 2:
        shifts = [[(0, 1), (1, 0)]]
    else:
        shifts = [[(i, i + 1) for i in range(cols - 1)], [(i + 1, i) for i in range(cols - 1)]]
    top, bottom, *rest = edges(object_field, margin, len(shifts))
    from_above = lax.ppermute(bottom, "row", downward)
    from_below = lax.ppermute(top, "row", upward)
    sides, corners = [], []
    for g, shift in enumerate(shifts):
        sides.append(lax.ppermute(rest[g], "col", shift))
        at = jnp.where(col == 0, tile - margin, 0) if cols == 2 else (tile - margin, 0)[g]
        ends = [lax.dynamic_slice_in_dim(strip, at, margin, 1) for strip in (from_above, from_below)]
        corners.append(lax.ppermute(jnp.stack(ends), "col", shift))
    strips = [from_above, from_below, sides[0], sides[-1], corners[0], corners[-1]]
    mine = cut_patches(offsets, object_field, strips, size, slots)
    sibling = [("mode", 0)] * 2
    other = swap(mine, sibling)

    spectrum, power = forward(probe_modes, mine, other, staged(tables))
    power_other = swap(power, sibling)
    col_dims = [("col", b) for b in range(cols.bit_length() - 1)]
    row_dims = [("row", b) for b in range(rows.bit_length() - 1)]
    x, z = col_dims[0], row_dims[0]
    rest = [(dim, dim) for dim in col_dims[1:] + row_dims[1:]]
    turns = {"A": [(x, x), (z, z)] + rest, "C": [(z, z), (x, x)] + rest, "S": [(x, z), (z, x)] + rest}
    plans = [turns[kind] for kind, _ in CHUNKS]
    sides = [crossed(plan[0])[1] for plan in plans]
    *planes, object_keep, object_send = backward(
        jnp.stack([counts[0, 0]] + sides), [chunk for _, chunk in CHUNKS], probe_modes, mine, other,
        amplitudes[0, 0], power, power_other, spectrum, tables, 1.0 / math.sqrt(rows * cols),
    )

    sums = [summed(*parts) for parts in zip(planes[0::2], planes[1::2], plans)]

    if cols == 2:
        out_starts = [jnp.where(col == 0, tile + margin, 0)]
        in_starts = [jnp.where(col == 0, tile - margin, 0)]
    else:
        out_starts = [jnp.int32(tile + margin), jnp.int32(0)]
        in_starts = [jnp.int32(0), jnp.int32(tile - margin)]
    columns, outgoing = place(
        jnp.concatenate([offsets, jnp.stack(out_starts)]), object_keep, swap(object_send, sibling), tile, len(shifts)
    )
    arrived = [lax.ppermute(outgoing[g], "col", shift) for g, shift in enumerate(shifts)]
    top, middle, bottom = merge(jnp.stack(in_starts), columns, arrived)
    above = lax.ppermute(bottom, "row", downward)
    below = lax.ppermute(top, "row", upward)
    object_grad = finish(middle, above, below)

    grads = {}
    for (own, back), side, (_, chunk) in zip(sums, sides, CHUNKS):
        low, high = jnp.where(side == 0, own, back), jnp.where(side == 0, back, own)
        for k, m in enumerate(chunk):
            grads[m] = jnp.stack([part[k * size : (k + 1) * size] for part in (low, high)])
    probe_grad = jnp.stack([grads[m] for m in range(modes)])
    return (object_grad, probe_grad)


def solution(mesh):
    return jax.shard_map(
        shards,
        mesh=mesh,
        in_specs=(
            P("scene", "row", "col"),
            P(("scene", "mode"), None, None, None),
            P(("scene", "row"), "col", None, None, None),
            P(("scene", "row"), "col", None, None),
            P(("scene", "row"), "col"),
        ),
        out_specs=(P(("scene", "mode"), "row", "col"), P(("scene", "mode"), None, None, None)),
        check_vma=False,
    )
```
